256 devices in a mesh: ep: 32 (over z, y), dp: 8 (over x, core).
Axes of the slice: x: 4, y: 4, z: 8, core: 2. Of those that a mesh axis runs over, the one named last changes fastest.
Arguments:
- tokens: bfloat16 [2048, 7168], P('ep', 'dp'), may hold values from -6 to 6
- gate_weight: bfloat16 [32, 7168, 2048], P('ep', None, 'dp'), may hold values from -0.0625 to 0.0625
- up_weight: bfloat16 [32, 7168, 2048], P('ep', None, 'dp'), may hold values from -0.0625 to 0.0625
- down_weight: bfloat16 [32, 2048, 7168], P('ep', None, 'dp'), may hold values from -0.125 to 0.125
- routes: int32 [2048, 8], P('ep'), may hold values from 0 to 31, all different within a row; in each aligned block of 64 rows (0 to 63, 64 to 127, ...) at most 20 rows name the same one
- route_weights: float32 [2048, 8], P('ep'), may hold values from 0.1 to 1
- slot_counts: int32 [2048], P('ep'), may hold values from 4 to 8
Outputs:
- mixed: bfloat16 [2048, 7168], P('ep', 'dp')
The draws below stay inside these ranges and needn't reach their ends.
Inputs may be any that keep to these rules, and one draw needn't show every extreme that they name: `routes`: each row names 8 different experts; of the 64 rows of one index of ep at most 20 name one expert.
All inputs are finite; a program needn't handle non-finite values.
Results may differ from the reference program's by a relative error of at most 0.0057.
Values may be sent and summed in bfloat16 or wider, within the bound.
A program may use at most 128 MiB of HBM per device.

```python
import math
import jax
import jax.numpy as jnp
import numpy as np
from jax import lax

D = 7168
FF = 2048
TOPK = 8
ROWS_DEV = 64
EXPERTS = 32
ROWS = 2048
CAP = 20
N_EP = 32


def plant(drawn, own_key, low, top_value):
    spot = [jax.random.randint(jax.random.fold_in(own_key, axis), (), 0, length) for axis, length in enumerate(drawn.shape)]
    widest = drawn.shape.index(max(drawn.shape))
    next_to = spot[:widest] + [(spot[widest] + 1) % drawn.shape[widest]] + spot[widest + 1:]
    return drawn.at[tuple(spot)].set(low).at[tuple(next_to)].set(top_value)


def block_levels(key, shape, split, low, high):
    gain, own = 1.0, jax.random.fold_in(key, 6)
    for axis_at, shards_of in split:
        draws = jnp.exp(jax.random.uniform(jax.random.fold_in(own, axis_at), (shards_of,), jnp.float32, low / len(split), high / len(split)))
        gain = gain * jnp.repeat(draws, shape[axis_at] // shards_of).reshape([-1 if axis == axis_at else 1 for axis in range(len(shape))])
    return gain


def shared_out(stream_key, own, number, rows, count, top, most, slope):
    ranking = jax.random.permutation(stream_key, count)
    packed, usual = portions_of(count, rows * top, most, slope, True), portions_of(count, rows * top, most, slope, False)
    places = jnp.arange(count)

    def named(lengths, rotation):
        used = int((lengths > 0).sum())
        fixed = max(1, used // 4)
        shifted = fixed + (places - fixed + rotation * (used - fixed)) % max(1, count - fixed)
        return jnp.zeros((count,), jnp.int32).at[ranking[jnp.where(places < fixed, places, shifted)]].set(jnp.asarray(lengths, jnp.int32))

    lengths = jnp.where(number % 4 == 0, named(packed, number // 4), named(usual, number - number // 4 - 1))
    mixed = jax.random.permutation(jax.random.fold_in(own, 3), count)
    source_of, receiver = mixed[0:count // 2 * 2:2], mixed[1:count // 2 * 2:2]
    margin = jnp.minimum(lengths[source_of] - 1, most - lengths[receiver]) // 2
    margin = jnp.where((source_of == ranking[0]) | (receiver == ranking[0]) | (lengths[receiver] == 0), 0, jnp.maximum(margin, 0))
    shifted = jax.random.randint(jax.random.fold_in(own, 4), (count // 2,), 0, 1 << 20) % (margin + 1)
    lengths = lengths.at[source_of].add(-shifted).at[receiver].add(shifted)
    items = jnp.searchsorted(jnp.cumsum(lengths), jnp.arange(rows * top), side="right").astype(jnp.int32)
    table = items.reshape(top, rows).T
    table = table[jax.random.permutation(jax.random.fold_in(own, 1), rows)]
    rotation = jax.random.randint(jax.random.fold_in(own, 2), (rows, 1), 0, top)
    return jnp.take_along_axis(table, (jnp.arange(top)[None, :] + rotation) % top, axis=1)


def portions_of(count, total, bound, skew, full):
    portions = [(1 << 20) // math.isqrt(grade ** skew) + 1 for grade in range(1, count + 1)]
    largest = bound if full else min(bound, max(-(-total // count), total * portions[0] // sum(portions)))
    least = 1 if total - largest >= count - 1 else 0
    holding, rest = [largest] + [least] * (count - 1), total - largest - least * (count - 1)
    while rest > 0:
        movable = [i for i in range(1, count) if holding[i] < largest] or [i for i in range(1, count) if holding[i] < bound]
        mass, budget = sum([portions[i] for i in movable]), rest
        for i in movable:
            addition = min(bound - holding[i], max(1, budget * portions[i] // mass), rest)
            holding[i] = holding[i] + addition
            rest = rest - addition
    return np.array(holding)


def scatter_about(own_key, dims, width, most, shards=(), kind=jnp.bfloat16):
    array = width * jax.random.normal(own_key, dims, jnp.float32)
    if shards:
        array = array * block_levels(own_key, dims, shards, -0.22, 0.18)
    return jnp.clip(array, -most, most).astype(kind)


def setup_inputs(seed: int = 0) -> dict:
    key_of = jax.random.split(jax.random.key(seed), 8)
    tokens = scatter_about(key_of[0], (ROWS, D), 1.0, 6.0, ((0, 32), (1, 8)))
    gate_weight = scatter_about(key_of[1], (EXPERTS, D, FF), D ** -0.5, 0.0625, ((0, 32), (2, 8)))
    up_weight = scatter_about(key_of[2], (EXPERTS, D, FF), D ** -0.5, 0.0625, ((0, 32), (2, 8)))
    down_weight = scatter_about(key_of[3], (EXPERTS, FF, D), FF ** -0.5, 0.125, ((0, 32), (2, 8)))
    routes_keys = jax.random.split(jax.random.fold_in(key_of[4], 1), ROWS // ROWS_DEV)
    routes_turns = jax.random.permutation(jax.random.fold_in(key_of[4], 3), ROWS // ROWS_DEV)
    routes = jax.vmap(lambda own, number: shared_out(jax.random.fold_in(key_of[4], 2), own, number, ROWS_DEV, EXPERTS, TOPK, CAP, 2))(routes_keys, routes_turns).reshape((ROWS, TOPK))
    route_weights = jnp.clip(jnp.exp(math.log(1.0) - 2.3025851 * jax.random.uniform(key_of[5], (ROWS, TOPK), jnp.float32) ** block_levels(key_of[5], (ROWS, TOPK), ((0, 32),), -0.2, 0.2)), 0.1, 1.0)
    slot_counts = plant(jax.random.randint(key_of[6], (ROWS,), 4, 9), jax.random.fold_in(key_of[6], 1), 4, 8).astype(jnp.int32)
    return {"tokens": tokens, "gate_weight": gate_weight, "up_weight": up_weight, "down_weight": down_weight, "routes": routes, "route_weights": route_weights, "slot_counts": slot_counts}


def targets(route_rows, count_rows, expert_count, capacity):
    row_count, pick_count = route_rows.shape
    active = lax.broadcasted_iota(jnp.int32, (row_count, pick_count), 1) < count_rows[:, None]
    flat_routes = route_rows.reshape(-1)
    live_mask = active.reshape(-1)
    one_hot = ((flat_routes[:, None] == lax.broadcasted_iota(jnp.int32, (1, expert_count), 1)) & live_mask[:, None]).astype(jnp.int32)
    before = jnp.cumsum(one_hot, axis=0) - one_hot
    position = jnp.sum(before * one_hot, axis=1)
    destination = jnp.where(live_mask, flat_routes * capacity + position, expert_count * capacity)
    return destination.reshape(row_count, pick_count).astype(jnp.int32), active


def block_targets(route_rows, count_rows):
    return targets(route_rows, count_rows, EXPERTS, CAP)


def reference(tokens, gate_weight, up_weight, down_weight, routes, route_weights, slot_counts):
    blocked = routes.reshape(N_EP, ROWS_DEV, TOPK)
    destination, active = jax.vmap(block_targets)(blocked, slot_counts.reshape(N_EP, ROWS_DEV))
    block_index = lax.broadcasted_iota(jnp.int32, (N_EP, ROWS_DEV, TOPK), 0)
    owner_row = block_index * ROWS_DEV + lax.broadcasted_iota(jnp.int32, (N_EP, ROWS_DEV, TOPK), 1)
    slot_table = jnp.full((N_EP, EXPERTS * CAP), -1, jnp.int32).at[block_index, destination].set(owner_row, mode="drop")
    slot_table = slot_table.reshape(N_EP, EXPERTS, CAP).transpose(1, 0, 2).reshape(EXPERTS, N_EP * CAP)
    live_weights = jnp.where(active.reshape(ROWS, TOPK), route_weights, jnp.float32(0.0))

    def expert_pass(accumulated, expert):
        slot_rows = slot_table[expert]
        occupied = slot_rows >= 0
        clipped = jnp.maximum(slot_rows, 0).astype(jnp.int32)
        inputs_e = jnp.where(occupied[:, None], tokens[clipped], jnp.zeros((), jnp.bfloat16))
        gate_act = jnp.dot(inputs_e, gate_weight[expert], preferred_element_type=jnp.float32)
        up_act = jnp.dot(inputs_e, up_weight[expert], preferred_element_type=jnp.float32)
        hidden = (jax.nn.silu(gate_act) * up_act).astype(jnp.bfloat16)
        output_e = jnp.dot(hidden, down_weight[expert], preferred_element_type=jnp.float32).astype(jnp.bfloat16)
        weight_e = jnp.sum(jnp.where(routes == expert, live_weights, jnp.float32(0.0)), axis=1)
        scaling = jnp.where(occupied, weight_e[clipped], jnp.float32(0.0))
        accumulated = accumulated.at[clipped].add(scaling[:, None] * output_e.astype(jnp.float32))
        return accumulated, None

    mixed, _ = lax.scan(expert_pass, jnp.zeros((ROWS, D), jnp.float32), jnp.arange(EXPERTS, dtype=jnp.int32))
    return mixed.astype(jnp.bfloat16)
```

```python
import jax
import jax.numpy as jnp
from jax import lax
from jax.experimental import pallas as pl
from jax.experimental.pallas import tpu as pltpu
from jax.sharding import PartitionSpec as P

MESH = pl.DeviceIdType.MESH
NZ, NY, NX = 8, 4, 4
CAP = 20
Q = NZ * CAP
MARK = 1024.0
ORDER = (0, 1, 3, 2)
F32 = jnp.float32
BF16 = jnp.bfloat16


def kernel(
    tokens, routes, weights, counts, gate, up, down, mixed,
    rows, table, gate_w, up_w, down_w, place_t, choose, choose_t, picked, gath, hid, outs, back, part,
    carry, came, load_sem, send, recv,
):
    row_count, width = tokens.shape
    units = gate_w.shape[1]
    top = routes.shape[1]
    all_rows = NZ * row_count
    ep, dp = lax.axis_index("ep"), lax.axis_index("dp")
    z, y, x, core = ep // NY, ep % NY, dp // 2, dp % 2
    used = [0]

    def at_z(k):
        return (((z + k) % NZ) * NY + y, dp)

    def at_y(k):
        return (z * NY + (y + k) % NY, dp)

    def at_x(k):
        return (ep, ((x + k) % NX) * 2 + core)

    other = (ep, x * 2 + 1 - core)

    def link(src, dst, device):
        n = used[0]
        used[0] += 1
        return pltpu.make_async_remote_copy(
            src_ref=src, dst_ref=dst, send_sem=send.at[n], recv_sem=recv.at[n],
            device_id=device, device_id_type=MESH,
        )

    sent = []

    def go(copy):
        copy.start()
        sent.append(copy)
        return copy

    loads = [
        pltpu.make_async_copy(gate.at[0], gate_w, load_sem.at[0]),
        pltpu.make_async_copy(up.at[0], up_w, load_sem.at[1]),
        pltpu.make_async_copy(down.at[0], down_w, load_sem.at[2]),
    ]
    for load in loads:
        load.start()

    barrier = pltpu.get_barrier_semaphore()
    partners = [at_z(k) for k in range(1, NZ)] + [at_y(k) for k in range(1, NY)] + [at_x(1), at_x(-1), other]
    for device in partners:
        pl.semaphore_signal(barrier, inc=1, device_id=device, device_id_type=MESH)

    lane = lax.broadcasted_iota(jnp.int32, (row_count, 128), 1)
    dense = jnp.zeros((row_count, 128), F32)
    for k in range(top):
        live = jnp.logical_and(lane == routes[:, k : k + 1], counts[...] > k)
        dense = dense + jnp.where(live, weights[:, k : k + 1], 0.0)
    table[pl.ds(0, row_count), :] = dense

    pl.semaphore_wait(barrier, len(partners))

    def block(ref, k):
        return ref.at[pl.ds(k * row_count, row_count)]

    half = NZ // 2
    down_going = {1: go(link(tokens, block(rows, 1), at_z(-1)))}
    up_going = {NZ - 1: go(link(tokens, block(rows, NZ - 1), at_z(1)))}
    tables = [go(link(block(table, 0), block(table, NZ - k), at_z(k))) for k in range(1, NZ)]
    rows[pl.ds(0, row_count), :] = tokens[...]

    for copy in tables:
        copy.wait_recv()
    taken = jnp.where(table[...] > 0.0, 1.0, 0.0).astype(BF16)
    first = lax.broadcasted_iota(jnp.int32, (all_rows, all_rows), 0)
    second = lax.broadcasted_iota(jnp.int32, (all_rows, all_rows), 1)
    ahead = jnp.where(first < second, 1.0, jnp.where(first == second, MARK, 0.0)).astype(BF16)
    place_t[...] = lax.dot_general(taken, ahead, (((0,), (0,)), ((), ())), preferred_element_type=F32)
    behind = jnp.where(second < first, 1.0, jnp.where(first == second, MARK, 0.0)).astype(BF16)
    place = jnp.dot(behind, taken, preferred_element_type=F32)
    lanes = lax.broadcasted_iota(jnp.int32, (all_rows, 128), 1)
    scales = []
    for j in range(NY):
        expert = z * NY + (y + j) % NY
        slot = lax.broadcasted_iota(jnp.int32, (Q, all_rows), 0).astype(F32) + MARK
        choose[j] = jnp.where(place_t[pl.ds(expert, 1), :] == slot, 1.0, 0.0).astype(BF16)
        own = lanes == expert
        column = jnp.sum(jnp.where(own, place, 0.0), axis=1, keepdims=True)
        slot_t = lax.broadcasted_iota(jnp.int32, (all_rows, Q), 1).astype(F32) + MARK
        choose_t[j] = jnp.where(column == slot_t, 1.0, 0.0).astype(BF16)

    for k in range(1, half + 1):
        down_going[k].wait_recv()
        if k < half:
            down_going[k + 1] = go(link(block(rows, k), block(rows, k + 1), at_z(-1)))
            m = NZ - k
            up_going[m].wait_recv()
            if m - 1 > half:
                up_going[m - 1] = go(link(block(rows, m), block(rows, m - 1), at_z(1)))

    to_expert = {}

    def pick(j):
        chosen = jnp.dot(choose[j], rows[...], preferred_element_type=F32).astype(BF16)
        if j == 0:
            gath[0, 0, 0] = chosen
        else:
            picked[j - 1] = chosen
            r = NY - j
            to_expert[r] = go(link(picked.at[j - 1], gath.at[r, 0, 0], at_y(j)))

    rings = {}

    def ring_a(buf, name, r):
        mine = buf.at[r, 0, 0]
        rings[name, r] = [
            go(link(mine, buf.at[r, 3, 0], at_x(1))),
            go(link(mine, buf.at[r, 1, 0], at_x(-1))),
            go(link(mine, buf.at[r, 0, 1], other)),
        ]

    def ring_b(buf, name, r):
        ring = rings[name, r]
        low, high = pl.ds(0, Q // 2), pl.ds(Q // 2, Q // 2)
        ring[0].wait_recv()
        ring.append(go(link(buf.at[r, 3, 0, low], buf.at[r, 2, 0, low], at_x(1))))
        ring.append(go(link(buf.at[r, 3, 0], buf.at[r, 3, 1], other)))
        ring[1].wait_recv()
        ring.append(go(link(buf.at[r, 1, 0, high], buf.at[r, 2, 0, high], at_x(-1))))
        ring.append(go(link(buf.at[r, 1, 0], buf.at[r, 1, 1], other)))

    def ring_c(buf, name, r):
        ring = rings[name, r]
        ring[3].wait_recv()
        ring[5].wait_recv()
        ring.append(go(link(buf.at[r, 2, 0], buf.at[r, 2, 1], other)))

    STEPS = ((0, 0, None), (3, 0, None), (1, 0, None), (0, 1, 2), (3, 1, 4), (1, 1, 6), (2, 0, None), (2, 1, 7))

    def slice_at(dx, dc):
        return ((x + dx) % NX) * 2 + (core if dc == 0 else 1 - core)

    def stage_a(r):
        if r != 0:
            to_expert[r].wait_recv()
        ring_a(gath, "g", r)

    def stage_b(r):
        ring_b(gath, "g", r)

    def stage_c(r):
        ring_c(gath, "g", r)
        gate_acc = jnp.zeros((Q, units), F32)
        up_acc = jnp.zeros((Q, units), F32)
        for dx, dc, awaited in STEPS:
            if awaited is not None:
                rings["g", r][awaited].wait_recv()
            at = pl.ds(pl.multiple_of(slice_at(dx, dc) * width, width), width)
            piece = gath[r, dx, dc]
            gate_acc = gate_acc + jnp.dot(piece, gate_w[at, :], preferred_element_type=F32)
            up_acc = up_acc + jnp.dot(piece, up_w[at, :], preferred_element_type=F32)
        hid[r, 0, 0] = (gate_acc / (1.0 + jnp.exp(-gate_acc)) * up_acc).astype(BF16)
        ring_a(hid, "h", r)

    def stage_d(r):
        ring_b(hid, "h", r)

    from_expert = {}

    def stage_e(r):
        ring_c(hid, "h", r)
        acc = jnp.zeros((Q, width), F32)
        for dx, dc, awaited in STEPS:
            if awaited is not None:
                rings["h", r][awaited].wait_recv()
            at = pl.ds(pl.multiple_of(slice_at(dx, dc) * units, units), units)
            acc = acc + jnp.dot(hid[r, dx, dc], down_w[at, :], preferred_element_type=F32)
        if r == 0:
            back[0] = acc.astype(BF16)
        else:
            outs[r - 1] = acc.astype(BF16)
            from_expert[NY - r] = go(link(outs.at[r - 1], back.at[NY - r], at_y(r)))

    a, b, c, d = ORDER
    pick(0)
    stage_a(0)
    for j in (1, 3, 2):
        pick(j)
    loads[0].wait()
    loads[1].wait()
    loads[2].wait()
    stage_a(b)
    stage_b(a)
    stage_a(c)
    stage_b(b)
    stage_c(a)
    stage_a(d)
    stage_b(c)
    stage_c(b)
    stage_d(a)
    stage_b(d)
    stage_c(c)
    stage_d(b)
    stage_e(a)
    stage_c(d)
    stage_d(c)
    stage_e(b)
    stage_d(d)
    stage_e(c)
    stage_e(d)

    for j in range(1, NY):
        from_expert[j].wait_recv()

    def weighted(k):
        span = pl.ds(k * row_count, row_count)
        total = jnp.zeros((row_count, width), F32)
        lanes_k = lax.broadcasted_iota(jnp.int32, (row_count, 128), 1)
        for j in range(NY):
            expert = z * NY + (y + j) % NY
            scale = jnp.sum(jnp.where(lanes_k == expert, table[span, :], 0.0), axis=1, keepdims=True)
            fetched = jnp.dot(choose_t[j, span, :], back[j], preferred_element_type=F32)
            total = total + scale * fetched
        return total

    part[half] = weighted(half).astype(BF16)
    up_sum = go(link(part.at[half], came.at[half - 1], at_z(1)))
    part[half + 1] = weighted(half + 1).astype(BF16)
    down_sum = go(link(part.at[half + 1], came.at[half + 1], at_z(-1)))
    for k in range(half - 1, 0, -1):
        mine = weighted(k)
        up_sum.wait_recv()
        part[k] = (mine + came[k].astype(F32)).astype(BF16)
        up_sum = go(link(part.at[k], came.at[k - 1], at_z(1)))
        m = NZ - k
        if m > half + 1:
            mine = weighted(m)
            down_sum.wait_recv()
            part[m] = (mine + came[m - 1].astype(F32)).astype(BF16)
            down_sum = go(link(part.at[m], came.at[m], at_z(-1)))
    mine = weighted(0)
    up_sum.wait_recv()
    down_sum.wait_recv()
    mixed[...] = (mine + came[0].astype(F32) + came[NZ - 1].astype(F32)).astype(BF16)
    for copy in sent:
        copy.wait_send()


COPIES = 96


def shards(tokens, gate_weight, up_weight, down_weight, routes, route_weights, slot_counts):
    row_count, width = tokens.shape
    _, depth, units = gate_weight.shape
    hidden = down_weight.shape[1]
    vmem = pl.BlockSpec(memory_space=pltpu.VMEM)
    hbm = pl.BlockSpec(memory_space=pl.ANY)
    all_rows = NZ * row_count
    return pl.pallas_call(
        kernel,
        out_shape=jax.ShapeDtypeStruct((row_count, width), BF16),
        in_specs=[vmem] * 4 + [hbm] * 3,
        out_specs=vmem,
        scratch_shapes=[
            pltpu.VMEM((all_rows, width), BF16),
            pltpu.VMEM((all_rows, 128), F32),
            pltpu.VMEM((depth, units), BF16),
            pltpu.VMEM((depth, units), BF16),
            pltpu.VMEM((hidden, width), BF16),
            pltpu.VMEM((128, all_rows), F32),
            pltpu.VMEM((NY, Q, all_rows), BF16),
            pltpu.VMEM((NY, all_rows, Q), BF16),
            pltpu.VMEM((NY - 1, Q, width), BF16),
            pltpu.VMEM((NY, NX, 2, Q, width), BF16),
            pltpu.VMEM((NY, NX, 2, Q, units), BF16),
            pltpu.VMEM((NY - 1, Q, width), BF16),
            pltpu.VMEM((NY, Q, width), BF16),
            pltpu.VMEM((NZ, row_count, width), BF16),
            pltpu.VMEM((8, 128), F32),
            pltpu.VMEM((NZ, row_count, width), BF16),
            pltpu.SemaphoreType.DMA((3,)),
            pltpu.SemaphoreType.DMA((COPIES,)),
            pltpu.SemaphoreType.DMA((COPIES,)),
        ],
        compiler_params=pltpu.CompilerParams(
            collective_id=0, has_side_effects=True, vmem_limit_bytes=60 * 1024 * 1024
        ),
    )(tokens, routes, route_weights, slot_counts[:, None], gate_weight, up_weight, down_weight)


def solution(mesh):
    placed = (
        P("ep", "dp"),
        P("ep", None, "dp"),
        P("ep", None, "dp"),
        P("ep", None, "dp"),
        P("ep", None),
        P("ep", None),
        P("ep"),
    )
    return jax.shard_map(
        shards, mesh=mesh, in_specs=placed, out_specs=P("ep", "dp"), check_vma=False
    )
```

```python
import jax
import jax.numpy as jnp
from jax import lax
from jax.experimental import pallas as pl
from jax.experimental.pallas import tpu as pltpu
from jax.sharding import PartitionSpec as P

MESH = pl.DeviceIdType.MESH
NZ, NY, NX = 8, 4, 4
CAP = 20
EXPERTS = 32
TAG = 128
GROUPS = ((0, 1, 7, 2), (6, 3, 5, 4))
BLOCKS = GROUPS[0] + GROUPS[1]
G = len(GROUPS)
PER = len(GROUPS[0])
Q = PER * CAP
SIDE = (0, 1, 3, 2)
MARK = 1024.0
DIRECT = ((0, 3), (0, 2))
F32 = jnp.float32
BF16 = jnp.bfloat16
SCHEDULE = (
    "z1", "z2", "p0", "a0", "p1", "p3", "p2", "z3", "b0", "a1", "z4", "p4", "a4", "p5", "p7", "p6", "c0",
    "b1", "a5", "m0", "c1", "b4", "a6", "e0", "m1", "c4", "b5", "a7", "f0", "e1", "m4", "c5", "b6", "a3",
    "f1", "e4", "m5", "c6", "b7", "a2", "f4", "e5", "m6", "c7", "b3", "f5", "e6", "m7", "c3", "b2", "f6",
    "e7", "m3", "f7", "c2", "e3", "m2", "f3", "s1", "e2", "f2", "s0", "s2",
)


def kernel(
    tokens, routes, weights, counts, gate, up, down, mixed,
    rows, gate_w, up_w, down_w, place_t, choose, choose_t, picked, gath, hid, outs, back, part, came,
    load_sem, send, recv,
):
    row_count, width = tokens.shape
    units = gate_w.shape[1]
    top = routes.shape[0]
    span = PER * row_count
    ep, dp = lax.axis_index("ep"), lax.axis_index("dp")
    z, y, x, core = ep // NY, ep % NY, dp // 2, dp % 2
    used = [0]
    sent = []

    def at_z(k):
        return (((z + k) % NZ) * NY + y, dp)

    def at_y(k):
        return (z * NY + (y + k) % NY, dp)

    def at_x(k):
        return (ep, ((x + k) % NX) * 2 + core)

    other = (ep, x * 2 + 1 - core)

    def go(src, dst, device):
        n = used[0]
        used[0] += 1
        copy = pltpu.make_async_remote_copy(
            src_ref=src, dst_ref=dst, send_sem=send.at[n], recv_sem=recv.at[n],
            device_id=device, device_id_type=MESH,
        )
        copy.start()
        sent.append(copy)
        return copy

    loads = [
        pltpu.make_async_copy(gate.at[0], gate_w, load_sem.at[0]),
        pltpu.make_async_copy(up.at[0], up_w, load_sem.at[1]),
        pltpu.make_async_copy(down.at[0], down_w, load_sem.at[2]),
    ]
    for load in loads:
        load.start()

    barrier = pltpu.get_barrier_semaphore()
    partners = [at_z(1), at_z(-1), at_z(2), at_z(-2), at_z(3), at_z(-3), at_x(2), at_y(1), at_y(2), at_y(3), at_x(1), at_x(-1), other]
    for device in partners:
        pl.semaphore_signal(barrier, inc=1, device_id=device, device_id_type=MESH)

    expert_at = lax.broadcasted_iota(jnp.int32, (TAG, row_count), 0) % EXPERTS
    dense = jnp.zeros((TAG, row_count), F32)
    for k in range(top):
        live = jnp.logical_and(expert_at == routes[k : k + 1, :], counts[...] > k)
        dense = dense + jnp.where(live, weights[k : k + 1, :], 0.0)
    dense = jnp.concatenate([dense, jnp.zeros((TAG, TAG - row_count), F32)], axis=1).T[:row_count]
    high = dense.astype(BF16).astype(F32)
    middle = (dense - high).astype(BF16).astype(F32)
    low = dense - high - middle
    term = lax.broadcasted_iota(jnp.int32, (row_count, TAG), 1) // EXPERTS
    tag = jnp.where(term == 0, high, jnp.where(term == 1, middle, jnp.where(term == 2, low, 0.0)))
    rows[pl.ds(0, row_count), pl.ds(width, TAG)] = tag.astype(BF16)
    rows[pl.ds(0, row_count), pl.ds(0, width)] = tokens[...]

    pl.semaphore_wait(barrier, len(partners))

    half_rows = row_count // 2

    def block(k, h):
        return rows.at[pl.ds(BLOCKS.index(k) * row_count + h * half_rows, half_rows)]

    moves = {}

    def onward(k, h, step):
        moves[(k + step) % NZ, h] = go(block(k, h), block((k + step) % NZ, h), at_z(-step))

    for h in (0, 1):
        onward(0, h, 1)
        onward(0, 1 - h, -1)

    def hop(k):
        for h in (0, 1):
            if k < NZ // 2:
                moves[k, h].wait_recv()
                if k < NZ // 2 - 1 or h == 0:
                    onward(k, h, 1)
                moves[NZ - k, 1 - h].wait_recv()
                if k < NZ // 2 - 1 or h == 0:
                    onward(NZ - k, 1 - h, -1)
            else:
                moves[k, h].wait_recv()

    def group_tags(g):
        return rows[pl.ds(g * span, span), pl.ds(width, TAG)]

    def places(g):
        taken = jnp.where(group_tags(g).astype(F32) > 0.0, 1.0, 0.0).astype(BF16)
        first = lax.broadcasted_iota(jnp.int32, (span, span), 0)
        second = lax.broadcasted_iota(jnp.int32, (span, span), 1)
        ahead = jnp.where(first < second, 1.0, jnp.where(first == second, MARK, 0.0)).astype(BF16)
        place_t[...] = lax.dot_general(taken, ahead, (((0,), (0,)), ((), ())), preferred_element_type=F32)
        behind = jnp.where(second < first, 1.0, jnp.where(first == second, MARK, 0.0)).astype(BF16)
        place = jnp.dot(behind, taken, preferred_element_type=F32)
        lanes = lax.broadcasted_iota(jnp.int32, (span, TAG), 1)
        slot = lax.broadcasted_iota(jnp.int32, (Q, span), 0).astype(F32) + MARK
        slot_t = lax.broadcasted_iota(jnp.int32, (span, Q), 1).astype(F32) + MARK
        for j in range(NY):
            expert = z * NY + (y + j) % NY
            choose[g, j] = jnp.where(place_t[pl.ds(expert, 1), :] == slot, 1.0, 0.0).astype(BF16)
            column = jnp.sum(jnp.where(lanes == expert, place, 0.0), axis=1, keepdims=True)
            choose_t[g, j] = jnp.where(column == slot_t, 1.0, 0.0).astype(BF16)

    def spot(q):
        return pl.ds(q * Q, Q)

    to_expert = {}

    def pick(g, j):
        if j == 0:
            places(g)
        source = rows[pl.ds(g * span, span), pl.ds(0, width)]
        chosen = jnp.dot(choose[g, j], source, preferred_element_type=F32).astype(BF16)
        q = SIDE.index((NY - j) % NY)
        if j == 0:
            gath[g, 0, 0, spot(q), :] = chosen
        else:
            picked[g, j - 1] = chosen
            to_expert[g, q] = go(picked.at[g, j - 1], gath.at[g, 0, 0, spot(q)], at_y(j))

    ring = {}

    def x_start(g, q):
        if (g, q) in to_expert:
            to_expert[g, q].wait_recv()
        at = spot(q)
        mine = gath.at[g, 0, 0, at]
        ring[g, q, 3, 0] = go(mine, gath.at[g, 3, 0, at], at_x(1))
        ring[g, q, 1, 0] = go(mine, gath.at[g, 1, 0, at], at_x(-1))
        ring[g, q, 0, 1] = go(mine, gath.at[g, 0, 1, at], other)

    def share(g, q, dx):
        at = spot(q)
        ring[g, q, dx, 1] = go(gath.at[g, dx, 0, at], gath.at[g, dx, 1, at], other)

    def x_forward(g, q):
        at = spot(q)
        ring[g, q, 3, 0].wait_recv()
        if q % 2 == 0:
            ring[g, q, 2, 0] = go(gath.at[g, 3, 0, at], gath.at[g, 2, 0, at], at_x(1))
        share(g, q, 3)
        ring[g, q, 1, 0].wait_recv()
        if q % 2 == 1:
            ring[g, q, 2, 0] = go(gath.at[g, 1, 0, at], gath.at[g, 2, 0, at], at_x(-1))
        share(g, q, 1)

    def x_last(g, q):
        ring[g, q, 2, 0].wait_recv()
        share(g, q, 2)

    STEPS = ((0, 0), (3, 0), (1, 0), (2, 0), (0, 1), (3, 1), (1, 1), (2, 1))
    waited = []

    def slice_at(dx, dc):
        return ((x + dx) % NX) * 2 + (core if dc == 0 else 1 - core)

    hops = {}

    def first_half(g, q):
        if not waited:
            waited.append(1)
            for load in loads:
                load.wait()
        at = spot(q)
        gate_acc = jnp.zeros((Q, units), F32)
        up_acc = jnp.zeros((Q, units), F32)
        for dx, dc in STEPS:
            if dc == 1:
                ring[g, q, dx, 1].wait_recv()
            deep = pl.ds(pl.multiple_of(slice_at(dx, dc) * width, width), width)
            piece = gath[g, dx, dc, at, :]
            gate_acc = gate_acc + jnp.dot(piece, gate_w[deep, :], preferred_element_type=F32)
            up_acc = up_acc + jnp.dot(piece, up_w[deep, :], preferred_element_type=F32)
        hid[g, 0, 0, at, :] = (gate_acc / (1.0 + jnp.exp(-gate_acc)) * up_acc).astype(BF16)
        mine = hid.at[g, 0, 0, at]
        hops[g, q, 3, 0] = go(mine, hid.at[g, 3, 0, at], at_x(1))
        hops[g, q, 1, 0] = go(mine, hid.at[g, 1, 0, at], at_x(-1))
        if (g, q) in DIRECT:
            hops[g, q, 2, 0] = go(mine, hid.at[g, 2, 0, at], at_x(2))
        hops[g, q, 0, 1] = go(mine, hid.at[g, 0, 1, at], other)

    def hidden_forward(g, q):
        at = spot(q)
        for dx, step in ((3, 1), (1, -1)):
            hops[g, q, dx, 0].wait_recv()
            if (g, q) not in DIRECT and q % 2 == (dx == 1):
                hops[g, q, 2, 0] = go(hid.at[g, dx, 0, at], hid.at[g, 2, 0, at], at_x(step))
            hops[g, q, dx, 1] = go(hid.at[g, dx, 0, at], hid.at[g, dx, 1, at], other)

    from_expert = {}

    def second_half(g, q):
        at = spot(q)
        hops[g, q, 2, 0].wait_recv()
        hops[g, q, 2, 1] = go(hid.at[g, 2, 0, at], hid.at[g, 2, 1, at], other)
        acc = jnp.zeros((Q, width), F32)
        for dx, dc in STEPS:
            if dc == 1:
                hops[g, q, dx, 1].wait_recv()
            deep = pl.ds(pl.multiple_of(slice_at(dx, dc) * units, units), units)
            acc = acc + jnp.dot(hid[g, dx, dc, at, :], down_w[deep, :], preferred_element_type=F32)
        r = SIDE[q]
        if r == 0:
            back[g, 0] = acc.astype(BF16)
        else:
            outs[g, r - 1] = acc.astype(BF16)
            from_expert[g, NY - r] = go(outs.at[g, r - 1], back.at[g, NY - r], at_y(r))

    def weighted(k):
        n = BLOCKS.index(k)
        g, at = n // PER, pl.ds(n % PER * row_count, row_count)
        tags = rows[pl.ds(n * row_count, row_count), pl.ds(width, TAG)].astype(F32)
        lanes = lax.broadcasted_iota(jnp.int32, (row_count, TAG), 1) % EXPERTS
        total = jnp.zeros((row_count, width), F32)
        for j in range(NY):
            expert = z * NY + (y + j) % NY
            scale = jnp.sum(jnp.where(lanes == expert, tags, 0.0), axis=1, keepdims=True)
            fetched = jnp.dot(choose_t[g, j, at, :], back[g, j], preferred_element_type=F32)
            total = total + scale * fetched
        return total

    def returned(g):
        for j in range(1, NY):
            from_expert[g, j].wait_recv()

    sums = {}

    def far_sums():
        returned(1)
        part[4] = weighted(4).astype(BF16)
        sums[3] = go(part.at[4], came.at[0], at_z(1))
        part[5] = weighted(5).astype(BF16)
        sums[6] = go(part.at[5], came.at[1], at_z(-1))
        mine = weighted(3)
        sums[3].wait_recv()
        part[3] = (mine + came[0].astype(F32)).astype(BF16)
        sums[0, 3] = go(part.at[3], came.at[2], at_z(3))
        mine = weighted(6)
        sums[6].wait_recv()
        part[6] = (mine + came[1].astype(F32)).astype(BF16)
        sums[0, 6] = go(part.at[6], came.at[3], at_z(-2))

    def near_sums():
        returned(0)
        part[2] = weighted(2).astype(BF16)
        sums[0, 2] = go(part.at[2], came.at[4], at_z(2))
        part[1] = weighted(1).astype(BF16)
        sums[0, 1] = go(part.at[1], came.at[5], at_z(1))
        part[7] = weighted(7).astype(BF16)
        sums[0, 7] = go(part.at[7], came.at[6], at_z(-1))

    def finish():
        total = weighted(0)
        for n, k in ((5, 1), (6, 7), (4, 2), (3, 6), (2, 3)):
            sums[0, k].wait_recv()
            total = total + came[n].astype(F32)
        mixed[...] = total.astype(BF16)

    stages = {
        "a": x_start, "b": x_forward, "c": x_last, "m": first_half, "e": hidden_forward, "f": second_half,
    }
    for word in SCHEDULE:
        kind, number = word[0], int(word[1:])
        if kind == "z":
            hop(number)
        elif kind == "p":
            pick(number // 4, number % 4)
        elif kind == "s":
            (near_sums, far_sums, finish)[number]()
        else:
            stages[kind](number // 4, number % 4)
    for copy in sent:
        copy.wait_send()


COPIES = 176


def shards(tokens, gate_weight, up_weight, down_weight, routes, route_weights, slot_counts):
    row_count, width = tokens.shape
    _, depth, units = gate_weight.shape
    hidden = down_weight.shape[1]
    vmem = pl.BlockSpec(memory_space=pltpu.VMEM)
    hbm = pl.BlockSpec(memory_space=pl.ANY)
    span = PER * row_count
    return pl.pallas_call(
        kernel,
        out_shape=jax.ShapeDtypeStruct((row_count, width), BF16),
        in_specs=[vmem] * 4 + [hbm] * 3,
        out_specs=vmem,
        scratch_shapes=[
            pltpu.VMEM((NZ * row_count, width + TAG), BF16),
            pltpu.VMEM((depth, units), BF16),
            pltpu.VMEM((depth, units), BF16),
            pltpu.VMEM((hidden, width), BF16),
            pltpu.VMEM((TAG, span), F32),
            pltpu.VMEM((G, NY, Q, span), BF16),
            pltpu.VMEM((G, NY, span, Q), BF16),
            pltpu.VMEM((G, NY - 1, Q, width), BF16),
            pltpu.VMEM((G, NX, 2, NY * Q, width), BF16),
            pltpu.VMEM((G, NX, 2, NY * Q, units), BF16),
            pltpu.VMEM((G, NY - 1, Q, width), BF16),
            pltpu.VMEM((G, NY, Q, width), BF16),
            pltpu.VMEM((NZ, row_count, width), BF16),
            pltpu.VMEM((NZ - 1, row_count, width), BF16),
            pltpu.SemaphoreType.DMA((3,)),
            pltpu.SemaphoreType.DMA((COPIES,)),
            pltpu.SemaphoreType.DMA((COPIES,)),
        ],
        compiler_params=pltpu.CompilerParams(
            collective_id=0, has_side_effects=True, vmem_limit_bytes=60 * 1024 * 1024
        ),
    )(tokens, routes.T, route_weights.T, slot_counts[None, :], gate_weight, up_weight, down_weight)


def solution(mesh):
    placed = (
        P("ep", "dp"),
        P("ep", None, "dp"),
        P("ep", None, "dp"),
        P("ep", None, "dp"),
        P("ep", None),
        P("ep", None),
        P("ep"),
    )
    return jax.shard_map(
        shards, mesh=mesh, in_specs=placed, out_specs=P("ep", "dp"), check_vma=False
    )
```

```python
import jax
import jax.numpy as jnp
from jax import lax
from jax.experimental import pallas as pl
from jax.experimental.pallas import tpu as pltpu
from jax.sharding import PartitionSpec as P

MESH = pl.DeviceIdType.MESH
NZ, NY, NX = 8, 4, 4
CAP = 20
EXPERTS = 32
TAG = 128
EARLY = 256
GROUPS = ((0, 1, 7, 2), (6, 3, 5, 4))
BLOCKS = GROUPS[0] + GROUPS[1]
G = len(GROUPS)
PER = len(GROUPS[0])
Q = PER * CAP
SIDE = (0, 1, 3, 2)
MARK = 1024.0
DIRECT = ((1, 2), (1, 3),)
RING_DIRECT = ()
F32 = jnp.float32
BF16 = jnp.bfloat16
SCHEDULE = (
    "g0", "z1", "g1", "z2", "p0", "p3", "p2", "p1", "a0", "g2", "q0", "q2", "q1", "q3", "h0", "a1", "z3",
    "b0", "a2", "a3", "g3", "z4", "p4", "p7", "p5", "p6", "b1", "h3", "c0", "g4", "q4", "q7", "q6", "q5",
    "a4", "h4", "m0", "b2", "h2", "h1", "b3", "c1", "a5", "m1", "b4", "e0", "a6", "c2", "c3", "h5", "m2",
    "b5", "m3", "e1", "h7", "h6", "c4", "a7", "d0", "m4", "f0", "b6", "c5", "e2", "m5", "d1", "e3", "f1",
    "b7", "e4", "d3", "c6", "f3", "d2", "e5", "m6", "d4", "c7", "f2", "f4", "d5", "m7", "e6", "f5", "d6",
    "f6", "e7", "s0", "d7", "f7", "s1", "s3", "s2",
)


def kernel(
    tokens, routes, weights, counts, gate, up, down, mixed,
    rows, early, gate_w, up_w, down_w, place_t, choose, choose_t, picked, picked_e, gath, gath_e, hid, outs, back, part, came,
    load_sem, send, recv,
):
    row_count, width = tokens.shape
    units = gate_w.shape[1]
    top = routes.shape[0]
    span = PER * row_count
    main = width - EARLY
    ep, dp = lax.axis_index("ep"), lax.axis_index("dp")
    z, y, x, core = ep // NY, ep % NY, dp // 2, dp % 2
    used = [0]
    sent = []

    def at_z(k):
        return (((z + k) % NZ) * NY + y, dp)

    def at_y(k):
        return (z * NY + (y + k) % NY, dp)

    def at_x(k):
        return (ep, ((x + k) % NX) * 2 + core)

    other = (ep, x * 2 + 1 - core)

    def go(src, dst, device):
        n = used[0]
        used[0] += 1
        copy = pltpu.make_async_remote_copy(
            src_ref=src, dst_ref=dst, send_sem=send.at[n], recv_sem=recv.at[n],
            device_id=device, device_id_type=MESH,
        )
        copy.start()
        sent.append(copy)
        return copy

    loads = [
        pltpu.make_async_copy(gate.at[0], gate_w, load_sem.at[0]),
        pltpu.make_async_copy(up.at[0], up_w, load_sem.at[1]),
        pltpu.make_async_copy(down.at[0], down_w, load_sem.at[2]),
    ]
    for load in loads:
        load.start()

    barrier = pltpu.get_barrier_semaphore()
    partners = [at_z(1), at_z(-1), at_z(2), at_z(-2), at_z(3), at_z(-3), at_x(2), at_y(1), at_y(2), at_y(3), at_x(1), at_x(-1), other]
    for device in partners:
        pl.semaphore_signal(barrier, inc=1, device_id=device, device_id_type=MESH)

    expert_at = lax.broadcasted_iota(jnp.int32, (TAG, row_count), 0) % EXPERTS
    dense = jnp.zeros((TAG, row_count), F32)
    for k in range(top):
        live = jnp.logical_and(expert_at == routes[k : k + 1, :], counts[...] > k)
        dense = dense + jnp.where(live, weights[k : k + 1, :], 0.0)
    dense = jnp.concatenate([dense, jnp.zeros((TAG, TAG - row_count), F32)], axis=1).T[:row_count]
    high = dense.astype(BF16).astype(F32)
    middle = (dense - high).astype(BF16).astype(F32)
    low = dense - high - middle
    term = lax.broadcasted_iota(jnp.int32, (row_count, TAG), 1) // EXPERTS
    tag = jnp.where(term == 0, high, jnp.where(term == 1, middle, jnp.where(term == 2, low, 0.0)))
    rows[pl.ds(0, row_count), pl.ds(main, TAG)] = tag.astype(BF16)
    rows[pl.ds(0, row_count), pl.ds(0, main)] = tokens[:, :main]
    early[pl.ds(0, row_count), pl.ds(0, EARLY)] = tokens[:, main:]

    pl.semaphore_wait(barrier, len(partners))

    half_rows = row_count // 2

    def block(ref, k, h):
        return ref.at[pl.ds(BLOCKS.index(k) * row_count + h * half_rows, half_rows)]

    moves = {}

    def onward(ref, name, k, h, step):
        to = (k + step) % NZ
        moves[name, to, h] = go(block(ref, k, h), block(ref, to, h), at_z(-step))

    def first_hop(ref, name):
        for h in (0, 1):
            onward(ref, name, 0, h, 1)
            onward(ref, name, 0, 1 - h, -1)

    def hop(ref, name, k):
        for h in (0, 1):
            moves[name, k, h].wait_recv()
            if k < NZ // 2:
                if k < NZ // 2 - 1 or h == 0:
                    onward(ref, name, k, h, 1)
                moves[name, NZ - k, 1 - h].wait_recv()
                if k < NZ // 2 - 1 or h == 0:
                    onward(ref, name, NZ - k, 1 - h, -1)

    first_hop(rows, "main")

    own_rows = pl.ds(0, row_count)

    def early_at(dx):
        return pl.ds(dx * EARLY, EARLY)

    own_early = early.at[own_rows, early_at(0)]
    gathered = [go(own_early, early.at[own_rows, early_at(NX - step)], at_x(step)) for step in (1, 3, 2)]

    def early_hop(k):
        if k == 0:
            for copy in gathered:
                copy.wait_recv()
            first_hop(early, "early")
        else:
            hop(early, "early", k)

    def group_tags(g):
        return rows[pl.ds(g * span, span), pl.ds(main, TAG)]

    def places(g):
        taken = jnp.where(group_tags(g).astype(F32) > 0.0, 1.0, 0.0).astype(BF16)
        first = lax.broadcasted_iota(jnp.int32, (span, span), 0)
        second = lax.broadcasted_iota(jnp.int32, (span, span), 1)
        ahead = jnp.where(first < second, 1.0, jnp.where(first == second, MARK, 0.0)).astype(BF16)
        place_t[...] = lax.dot_general(taken, ahead, (((0,), (0,)), ((), ())), preferred_element_type=F32)
        behind = jnp.where(second < first, 1.0, jnp.where(first == second, MARK, 0.0)).astype(BF16)
        place = jnp.dot(behind, taken, preferred_element_type=F32)
        lanes = lax.broadcasted_iota(jnp.int32, (span, TAG), 1)
        slot = lax.broadcasted_iota(jnp.int32, (Q, span), 0).astype(F32) + MARK
        slot_t = lax.broadcasted_iota(jnp.int32, (span, Q), 1).astype(F32) + MARK
        for j in range(NY):
            expert = z * NY + (y + j) % NY
            choose[g, j] = jnp.where(place_t[pl.ds(expert, 1), :] == slot, 1.0, 0.0).astype(BF16)
            column = jnp.sum(jnp.where(lanes == expert, place, 0.0), axis=1, keepdims=True)
            choose_t[g, j] = jnp.where(column == slot_t, 1.0, 0.0).astype(BF16)

    def spot(q):
        return pl.ds(q * Q, Q)

    to_expert = {}

    def pick(g, j):
        if j == 0:
            places(g)
        source = rows[pl.ds(g * span, span), pl.ds(0, main)]
        chosen = jnp.dot(choose[g, j], source, preferred_element_type=F32).astype(BF16)
        q = SIDE.index((NY - j) % NY)
        if j == 0:
            gath[g, 0, 0, spot(q), :] = chosen
        else:
            picked[g, j - 1] = chosen
            to_expert[g, q] = go(picked.at[g, j - 1], gath.at[g, 0, 0, spot(q)], at_y(j))

    early_to = {}
    early_shared = {}

    def pick_early(g, j):
        chosen = jnp.dot(choose[g, j], early[pl.ds(g * span, span), :], preferred_element_type=F32).astype(BF16)
        q = SIDE.index((NY - j) % NY)
        if j == 0:
            gath_e[g, 0, spot(q), :] = chosen
        else:
            picked_e[g, j - 1] = chosen
            early_to[g, q] = go(picked_e.at[g, j - 1], gath_e.at[g, 0, spot(q)], at_y(j))

    def early_share(g, q):
        if (g, q) in early_to:
            early_to[g, q].wait_recv()
        early_shared[g, q] = go(gath_e.at[g, 0, spot(q)], gath_e.at[g, 1, spot(q)], other)

    ring = {}

    def x_start(g, q):
        if (g, q) in to_expert:
            to_expert[g, q].wait_recv()
        at = spot(q)
        mine = gath.at[g, 0, 0, at]
        ring[g, q, 3, 0] = go(mine, gath.at[g, 3, 0, at], at_x(1))
        ring[g, q, 1, 0] = go(mine, gath.at[g, 1, 0, at], at_x(-1))
        if (g, q) in RING_DIRECT:
            ring[g, q, 2, 0] = go(mine, gath.at[g, 2, 0, at], at_x(2))
        ring[g, q, 0, 1] = go(mine, gath.at[g, 0, 1, at], other)

    def share(g, q, dx):
        at = spot(q)
        ring[g, q, dx, 1] = go(gath.at[g, dx, 0, at], gath.at[g, dx, 1, at], other)

    def x_forward(g, q):
        at = spot(q)
        ring[g, q, 3, 0].wait_recv()
        if (g, q) not in RING_DIRECT and q % 2 == 0:
            ring[g, q, 2, 0] = go(gath.at[g, 3, 0, at], gath.at[g, 2, 0, at], at_x(1))
        share(g, q, 3)
        ring[g, q, 1, 0].wait_recv()
        if (g, q) not in RING_DIRECT and q % 2 == 1:
            ring[g, q, 2, 0] = go(gath.at[g, 1, 0, at], gath.at[g, 2, 0, at], at_x(-1))
        share(g, q, 1)

    def x_last(g, q):
        ring[g, q, 2, 0].wait_recv()
        share(g, q, 2)

    STEPS = ((0, 0), (3, 0), (1, 0), (2, 0), (0, 1), (3, 1), (1, 1), (2, 1))
    waited = []

    def slice_at(dx, dc):
        return ((x + dx) % NX) * 2 + (core if dc == 0 else 1 - core)

    hops = {}

    def first_half(g, q):
        if not waited:
            waited.append(1)
            for load in loads:
                load.wait()
        at = spot(q)
        early_shared[g, q].wait_recv()
        gate_acc = jnp.zeros((Q, units), F32)
        up_acc = jnp.zeros((Q, units), F32)
        for dx, dc in STEPS:
            deep = pl.ds(pl.multiple_of(slice_at(dx, dc) * width + main, EARLY // 2), EARLY)
            piece = gath_e[g, dc, at, early_at(dx)]
            gate_acc = gate_acc + jnp.dot(piece, gate_w[deep, :], preferred_element_type=F32)
            up_acc = up_acc + jnp.dot(piece, up_w[deep, :], preferred_element_type=F32)
        for dx, dc in STEPS:
            if dc == 1:
                ring[g, q, dx, 1].wait_recv()
            deep = pl.ds(pl.multiple_of(slice_at(dx, dc) * width, width), main)
            piece = gath[g, dx, dc, at, :]
            gate_acc = gate_acc + jnp.dot(piece, gate_w[deep, :], preferred_element_type=F32)
            up_acc = up_acc + jnp.dot(piece, up_w[deep, :], preferred_element_type=F32)
        hid[g, 0, 0, at, :] = (gate_acc / (1.0 + jnp.exp(-gate_acc)) * up_acc).astype(BF16)
        mine = hid.at[g, 0, 0, at]
        hops[g, q, 3, 0] = go(mine, hid.at[g, 3, 0, at], at_x(1))
        hops[g, q, 1, 0] = go(mine, hid.at[g, 1, 0, at], at_x(-1))
        if (g, q) in DIRECT:
            hops[g, q, 2, 0] = go(mine, hid.at[g, 2, 0, at], at_x(2))
        hops[g, q, 0, 1] = go(mine, hid.at[g, 0, 1, at], other)

    def hidden_forward(g, q):
        at = spot(q)
        for dx, step in ((3, 1), (1, -1)):
            hops[g, q, dx, 0].wait_recv()
            if (g, q) not in DIRECT and q % 2 == (dx == 1):
                hops[g, q, 2, 0] = go(hid.at[g, dx, 0, at], hid.at[g, 2, 0, at], at_x(step))
            hops[g, q, dx, 1] = go(hid.at[g, dx, 0, at], hid.at[g, dx, 1, at], other)

    def hidden_last(g, q):
        at = spot(q)
        hops[g, q, 2, 0].wait_recv()
        hops[g, q, 2, 1] = go(hid.at[g, 2, 0, at], hid.at[g, 2, 1, at], other)

    from_expert = {}

    def second_half(g, q):
        at = spot(q)
        acc = jnp.zeros((Q, width), F32)
        for dx, dc in STEPS:
            if dc == 1:
                hops[g, q, dx, 1].wait_recv()
            deep = pl.ds(pl.multiple_of(slice_at(dx, dc) * units, units), units)
            acc = acc + jnp.dot(hid[g, dx, dc, at, :], down_w[deep, :], preferred_element_type=F32)
        r = SIDE[q]
        if r == 0:
            back[g, 0] = acc.astype(BF16)
        else:
            outs[g, r - 1] = acc.astype(BF16)
            from_expert[g, NY - r] = go(outs.at[g, r - 1], back.at[g, NY - r], at_y(r))

    def weighted(k):
        n = BLOCKS.index(k)
        g, at = n // PER, pl.ds(n % PER * row_count, row_count)
        tags = rows[pl.ds(n * row_count, row_count), pl.ds(main, TAG)].astype(F32)
        lanes = lax.broadcasted_iota(jnp.int32, (row_count, TAG), 1) % EXPERTS
        total = jnp.zeros((row_count, width), F32)
        for j in range(NY):
            expert = z * NY + (y + j) % NY
            scale = jnp.sum(jnp.where(lanes == expert, tags, 0.0), axis=1, keepdims=True)
            fetched = jnp.dot(choose_t[g, j, at, :], back[g, j], preferred_element_type=F32)
            total = total + scale * fetched
        return total

    def returned(g):
        for j in range(1, NY):
            from_expert[g, j].wait_recv()

    sums = {}

    def far_sums():
        returned(1)
        part[4] = weighted(4).astype(BF16)
        sums[3] = go(part.at[4], came.at[0], at_z(1))
        part[5] = weighted(5).astype(BF16)
        sums[6] = go(part.at[5], came.at[1], at_z(-1))

    def far_ends():
        mine = weighted(3)
        sums[3].wait_recv()
        part[3] = (mine + came[0].astype(F32)).astype(BF16)
        sums[0, 3] = go(part.at[3], came.at[2], at_z(3))
        mine = weighted(6)
        sums[6].wait_recv()
        part[6] = (mine + came[1].astype(F32)).astype(BF16)
        sums[0, 6] = go(part.at[6], came.at[3], at_z(-2))

    def near_sums():
        returned(0)
        part[2] = weighted(2).astype(BF16)
        sums[0, 2] = go(part.at[2], came.at[4], at_z(2))
        part[1] = weighted(1).astype(BF16)
        sums[0, 1] = go(part.at[1], came.at[5], at_z(1))
        part[7] = weighted(7).astype(BF16)
        sums[0, 7] = go(part.at[7], came.at[6], at_z(-1))

    def finish():
        total = weighted(0)
        for n, k in ((5, 1), (6, 7), (4, 2), (3, 6), (2, 3)):
            sums[0, k].wait_recv()
            total = total + came[n].astype(F32)
        mixed[...] = total.astype(BF16)

    stages = {
        "q": pick_early, "h": early_share, "a": x_start, "b": x_forward, "c": x_last, "m": first_half, "e": hidden_forward,
        "d": hidden_last, "f": second_half,
    }
    for word in SCHEDULE:
        kind, number = word[0], int(word[1:])
        if kind == "z":
            hop(rows, "main", number)
        elif kind == "g":
            early_hop(number)
        elif kind == "p":
            pick(number // 4, number % 4)
        elif kind == "s":
            (near_sums, far_sums, finish, far_ends)[number]()
        else:
            stages[kind](number // 4, number % 4)
    for copy in sent:
        copy.wait_send()


COPIES = 220


def shards(tokens, gate_weight, up_weight, down_weight, routes, route_weights, slot_counts):
    row_count, width = tokens.shape
    _, depth, units = gate_weight.shape
    hidden = down_weight.shape[1]
    vmem = pl.BlockSpec(memory_space=pltpu.VMEM)
    hbm = pl.BlockSpec(memory_space=pl.ANY)
    span = PER * row_count
    main = width - EARLY
    return pl.pallas_call(
        kernel,
        out_shape=jax.ShapeDtypeStruct((row_count, width), BF16),
        in_specs=[vmem] * 4 + [hbm] * 3,
        out_specs=vmem,
        scratch_shapes=[
            pltpu.VMEM((NZ * row_count, main + TAG), BF16),
            pltpu.VMEM((NZ * row_count, NX * EARLY), BF16),
            pltpu.VMEM((depth, units), BF16),
            pltpu.VMEM((depth, units), BF16),
            pltpu.VMEM((hidden, width), BF16),
            pltpu.VMEM((TAG, span), F32),
            pltpu.VMEM((G, NY, Q, span), BF16),
            pltpu.VMEM((G, NY, span, Q), BF16),
            pltpu.VMEM((G, NY - 1, Q, main), BF16),
            pltpu.VMEM((G, NY - 1, Q, NX * EARLY), BF16),
            pltpu.VMEM((G, NX, 2, NY * Q, main), BF16),
            pltpu.VMEM((G, 2, NY * Q, NX * EARLY), BF16),
            pltpu.VMEM((G, NX, 2, NY * Q, units), BF16),
            pltpu.VMEM((G, NY - 1, Q, width), BF16),
            pltpu.VMEM((G, NY, Q, width), BF16),
            pltpu.VMEM((NZ, row_count, width), BF16),
            pltpu.VMEM((NZ - 1, row_count, width), BF16),
            pltpu.SemaphoreType.DMA((3,)),
            pltpu.SemaphoreType.DMA((COPIES,)),
            pltpu.SemaphoreType.DMA((COPIES,)),
        ],
        compiler_params=pltpu.CompilerParams(
            collective_id=0, has_side_effects=True, vmem_limit_bytes=60 * 1024 * 1024
        ),
    )(tokens, routes.T, route_weights.T, slot_counts[None, :], gate_weight, up_weight, down_weight)


def solution(mesh):
    placed = (
        P("ep", "dp"),
        P("ep", None, "dp"),
        P("ep", None, "dp"),
        P("ep", None, "dp"),
        P("ep", None),
        P("ep", None),
        P("ep"),
    )
    return jax.shard_map(
        shards, mesh=mesh, in_specs=placed, out_specs=P("ep", "dp"), check_vma=False
    )
```

```python
import jax
import jax.numpy as jnp
from jax import lax
from jax.experimental import pallas as pl
from jax.experimental.pallas import tpu as pltpu
from jax.sharding import PartitionSpec as P

MESH = pl.DeviceIdType.MESH
NZ, NY, NX = 8, 4, 4
CAP = 20
EXPERTS = 32
TAG = 128
EARLY = 256
GROUPS = ((0, 1, 7, 2), (6, 3, 5, 4))
BLOCKS = GROUPS[0] + GROUPS[1]
G = len(GROUPS)
PER = len(GROUPS[0])
Q = PER * CAP
SIDE = (0, 1, 3, 2)
MARK = 1024.0
COLUMNS = ((0, 512), (512, 384))
DIRECT = ((1, 2), (1, 3),)
RING_DIRECT = ()
F32 = jnp.float32
BF16 = jnp.bfloat16
SCHEDULE = (
    "g0", "z1", "g1", "z2", "p0", "p3", "p2", "p1", "a0", "g2", "q0", "q2", "q1", "q3", "h0", "a1", "z3",
    "b0", "a2", "a3", "g3", "z4", "p4", "p7", "p5", "p6", "b1", "h3", "c0", "g4", "q4", "q7", "q6", "q5",
    "a4", "h4", "m0", "b2", "h2", "h1", "b3", "c1", "a5", "m1", "b4", "e0", "a6", "c2", "c3", "h5", "m2",
    "b5", "m3", "e1", "h7", "h6", "c4", "a7", "d0", "m4", "f0", "b6", "c5", "e2", "m5", "d1", "e3", "f1",
    "b7", "e4", "d3", "c6", "f3", "d2", "e5", "m6", "d4", "c7", "f2", "f4", "d5", "m7", "e6", "f5", "d6",
    "f6", "e7", "s0", "d7", "f7", "s1", "s4", "s3", "s5", "s2",
)


def kernel(
    tokens, routes, weights, counts, gate, up, down, mixed,
    rows, early, gate_w, up_w, down_w, place_t, choose, choose_t, picked, picked_e, gath, gath_e, hid, outs, back, part, came,
    load_sem, send, recv,
):
    row_count, width = tokens.shape
    units = gate_w.shape[1]
    top = routes.shape[0]
    span = PER * row_count
    main = width - EARLY
    ep, dp = lax.axis_index("ep"), lax.axis_index("dp")
    z, y, x, core = ep // NY, ep % NY, dp // 2, dp % 2
    used = [0]
    sent = []

    def at_z(k):
        return (((z + k) % NZ) * NY + y, dp)

    def at_y(k):
        return (z * NY + (y + k) % NY, dp)

    def at_x(k):
        return (ep, ((x + k) % NX) * 2 + core)

    other = (ep, x * 2 + 1 - core)

    def go(src, dst, device):
        n = used[0]
        used[0] += 1
        copy = pltpu.make_async_remote_copy(
            src_ref=src, dst_ref=dst, send_sem=send.at[n], recv_sem=recv.at[n],
            device_id=device, device_id_type=MESH,
        )
        copy.start()
        sent.append(copy)
        return copy

    loads = [
        pltpu.make_async_copy(gate.at[0], gate_w, load_sem.at[0]),
        pltpu.make_async_copy(up.at[0], up_w, load_sem.at[1]),
        pltpu.make_async_copy(down.at[0], down_w, load_sem.at[2]),
    ]
    for load in loads:
        load.start()

    barrier = pltpu.get_barrier_semaphore()
    partners = [at_z(1), at_z(-1), at_z(2), at_z(-2), at_z(3), at_z(-3), at_x(2), at_y(1), at_y(2), at_y(3), at_x(1), at_x(-1), other]
    for device in partners:
        pl.semaphore_signal(barrier, inc=1, device_id=device, device_id_type=MESH)

    expert_at = lax.broadcasted_iota(jnp.int32, (TAG, row_count), 0) % EXPERTS
    dense = jnp.zeros((TAG, row_count), F32)
    for k in range(top):
        live = jnp.logical_and(expert_at == routes[k : k + 1, :], counts[...] > k)
        dense = dense + jnp.where(live, weights[k : k + 1, :], 0.0)
    dense = jnp.concatenate([dense, jnp.zeros((TAG, TAG - row_count), F32)], axis=1).T[:row_count]
    high = dense.astype(BF16).astype(F32)
    middle = (dense - high).astype(BF16).astype(F32)
    low = dense - high - middle
    term = lax.broadcasted_iota(jnp.int32, (row_count, TAG), 1) // EXPERTS
    tag = jnp.where(term == 0, high, jnp.where(term == 1, middle, jnp.where(term == 2, low, 0.0)))
    rows[pl.ds(0, row_count), pl.ds(main, TAG)] = tag.astype(BF16)
    rows[pl.ds(0, row_count), pl.ds(0, main)] = tokens[:, :main]
    early[pl.ds(0, row_count), pl.ds(0, EARLY)] = tokens[:, main:]

    pl.semaphore_wait(barrier, len(partners))

    half_rows = row_count // 2

    def block(ref, k, h):
        return ref.at[pl.ds(BLOCKS.index(k) * row_count + h * half_rows, half_rows)]

    moves = {}

    def onward(ref, name, k, h, step):
        to = (k + step) % NZ
        moves[name, to, h] = go(block(ref, k, h), block(ref, to, h), at_z(-step))

    def first_hop(ref, name):
        for h in (0, 1):
            onward(ref, name, 0, h, 1)
            onward(ref, name, 0, 1 - h, -1)

    def hop(ref, name, k):
        for h in (0, 1):
            moves[name, k, h].wait_recv()
            if k < NZ // 2:
                if k < NZ // 2 - 1 or h == 0:
                    onward(ref, name, k, h, 1)
                moves[name, NZ - k, 1 - h].wait_recv()
                if k < NZ // 2 - 1 or h == 0:
                    onward(ref, name, NZ - k, 1 - h, -1)

    first_hop(rows, "main")

    own_rows = pl.ds(0, row_count)

    def early_at(dx):
        return pl.ds(dx * EARLY, EARLY)

    own_early = early.at[own_rows, early_at(0)]
    gathered = [go(own_early, early.at[own_rows, early_at(NX - step)], at_x(step)) for step in (1, 3, 2)]

    def early_hop(k):
        if k == 0:
            for copy in gathered:
                copy.wait_recv()
            first_hop(early, "early")
        else:
            hop(early, "early", k)

    def group_tags(g):
        return rows[pl.ds(g * span, span), pl.ds(main, TAG)]

    def places(g):
        taken = jnp.where(group_tags(g).astype(F32) > 0.0, 1.0, 0.0).astype(BF16)
        first = lax.broadcasted_iota(jnp.int32, (span, span), 0)
        second = lax.broadcasted_iota(jnp.int32, (span, span), 1)
        ahead = jnp.where(first < second, 1.0, jnp.where(first == second, MARK, 0.0)).astype(BF16)
        place_t[...] = lax.dot_general(taken, ahead, (((0,), (0,)), ((), ())), preferred_element_type=F32)
        behind = jnp.where(second < first, 1.0, jnp.where(first == second, MARK, 0.0)).astype(BF16)
        place = jnp.dot(behind, taken, preferred_element_type=F32)
        lanes = lax.broadcasted_iota(jnp.int32, (span, TAG), 1)
        slot = lax.broadcasted_iota(jnp.int32, (Q, span), 0).astype(F32) + MARK
        slot_t = lax.broadcasted_iota(jnp.int32, (span, Q), 1).astype(F32) + MARK
        for j in range(NY):
            expert = z * NY + (y + j) % NY
            choose[g, j] = jnp.where(place_t[pl.ds(expert, 1), :] == slot, 1.0, 0.0).astype(BF16)
            column = jnp.sum(jnp.where(lanes == expert, place, 0.0), axis=1, keepdims=True)
            choose_t[g, j] = jnp.where(column == slot_t, 1.0, 0.0).astype(BF16)

    def spot(q):
        return pl.ds(q * Q, Q)

    to_expert = {}

    def pick(g, j):
        if j == 0:
            places(g)
        source = rows[pl.ds(g * span, span), pl.ds(0, main)]
        chosen = jnp.dot(choose[g, j], source, preferred_element_type=F32).astype(BF16)
        q = SIDE.index((NY - j) % NY)
        if j == 0:
            gath[g, 0, 0, spot(q), :] = chosen
        else:
            picked[g, j - 1] = chosen
            to_expert[g, q] = go(picked.at[g, j - 1], gath.at[g, 0, 0, spot(q)], at_y(j))

    early_to = {}
    early_shared = {}

    def pick_early(g, j):
        chosen = jnp.dot(choose[g, j], early[pl.ds(g * span, span), :], preferred_element_type=F32).astype(BF16)
        q = SIDE.index((NY - j) % NY)
        if j == 0:
            gath_e[g, 0, spot(q), :] = chosen
        else:
            picked_e[g, j - 1] = chosen
            early_to[g, q] = go(picked_e.at[g, j - 1], gath_e.at[g, 0, spot(q)], at_y(j))

    def early_share(g, q):
        if (g, q) in early_to:
            early_to[g, q].wait_recv()
        early_shared[g, q] = go(gath_e.at[g, 0, spot(q)], gath_e.at[g, 1, spot(q)], other)

    ring = {}

    def x_start(g, q):
        if (g, q) in to_expert:
            to_expert[g, q].wait_recv()
        at = spot(q)
        mine = gath.at[g, 0, 0, at]
        ring[g, q, 3, 0] = go(mine, gath.at[g, 3, 0, at], at_x(1))
        ring[g, q, 1, 0] = go(mine, gath.at[g, 1, 0, at], at_x(-1))
        if (g, q) in RING_DIRECT:
            ring[g, q, 2, 0] = go(mine, gath.at[g, 2, 0, at], at_x(2))
        ring[g, q, 0, 1] = go(mine, gath.at[g, 0, 1, at], other)

    def share(g, q, dx):
        at = spot(q)
        ring[g, q, dx, 1] = go(gath.at[g, dx, 0, at], gath.at[g, dx, 1, at], other)

    def x_forward(g, q):
        at = spot(q)
        ring[g, q, 3, 0].wait_recv()
        if (g, q) not in RING_DIRECT and q % 2 == 0:
            ring[g, q, 2, 0] = go(gath.at[g, 3, 0, at], gath.at[g, 2, 0, at], at_x(1))
        share(g, q, 3)
        ring[g, q, 1, 0].wait_recv()
        if (g, q) not in RING_DIRECT and q % 2 == 1:
            ring[g, q, 2, 0] = go(gath.at[g, 1, 0, at], gath.at[g, 2, 0, at], at_x(-1))
        share(g, q, 1)

    def x_last(g, q):
        ring[g, q, 2, 0].wait_recv()
        share(g, q, 2)

    STEPS = ((0, 0), (3, 0), (1, 0), (2, 0), (0, 1), (3, 1), (1, 1), (2, 1))
    waited = []

    def slice_at(dx, dc):
        return ((x + dx) % NX) * 2 + (core if dc == 0 else 1 - core)

    hops = {}

    def first_half(g, q):
        if not waited:
            waited.append(1)
            for load in loads:
                load.wait()
        at = spot(q)
        early_shared[g, q].wait_recv()
        gate_acc = jnp.zeros((Q, units), F32)
        up_acc = jnp.zeros((Q, units), F32)
        for dx, dc in STEPS:
            deep = pl.ds(pl.multiple_of(slice_at(dx, dc) * width + main, 128), EARLY)
            piece = gath_e[g, dc, at, early_at(dx)]
            gate_acc = gate_acc + jnp.dot(piece, gate_w[deep, :], preferred_element_type=F32)
            up_acc = up_acc + jnp.dot(piece, up_w[deep, :], preferred_element_type=F32)
        for dx, dc in STEPS:
            if dc == 1:
                ring[g, q, dx, 1].wait_recv()
            deep = pl.ds(pl.multiple_of(slice_at(dx, dc) * width, width), main)
            piece = gath[g, dx, dc, at, :]
            gate_acc = gate_acc + jnp.dot(piece, gate_w[deep, :], preferred_element_type=F32)
            up_acc = up_acc + jnp.dot(piece, up_w[deep, :], preferred_element_type=F32)
        hid[g, 0, 0, at, :] = (gate_acc / (1.0 + jnp.exp(-gate_acc)) * up_acc).astype(BF16)
        mine = hid.at[g, 0, 0, at]
        hops[g, q, 3, 0] = go(mine, hid.at[g, 3, 0, at], at_x(1))
        hops[g, q, 1, 0] = go(mine, hid.at[g, 1, 0, at], at_x(-1))
        if (g, q) in DIRECT:
            hops[g, q, 2, 0] = go(mine, hid.at[g, 2, 0, at], at_x(2))
        hops[g, q, 0, 1] = go(mine, hid.at[g, 0, 1, at], other)

    def hidden_forward(g, q):
        at = spot(q)
        for dx, step in ((3, 1), (1, -1)):
            hops[g, q, dx, 0].wait_recv()
            if (g, q) not in DIRECT and q % 2 == (dx == 1):
                hops[g, q, 2, 0] = go(hid.at[g, dx, 0, at], hid.at[g, 2, 0, at], at_x(step))
            hops[g, q, dx, 1] = go(hid.at[g, dx, 0, at], hid.at[g, dx, 1, at], other)

    def hidden_last(g, q):
        at = spot(q)
        hops[g, q, 2, 0].wait_recv()
        hops[g, q, 2, 1] = go(hid.at[g, 2, 0, at], hid.at[g, 2, 1, at], other)

    from_expert = {}

    def second_half(g, q):
        at = spot(q)
        acc = jnp.zeros((Q, width), F32)
        for dx, dc in STEPS:
            if dc == 1:
                hops[g, q, dx, 1].wait_recv()
            deep = pl.ds(pl.multiple_of(slice_at(dx, dc) * units, units), units)
            acc = acc + jnp.dot(hid[g, dx, dc, at, :], down_w[deep, :], preferred_element_type=F32)
        r = SIDE[q]
        if r == 0:
            back[g, 0] = acc.astype(BF16)
        else:
            outs[g, r - 1] = acc.astype(BF16)
            for n, columns in enumerate(COLUMNS):
                cut = pl.ds(0, Q), pl.ds(*columns)
                from_expert[g, NY - r, n] = go(
                    outs.at[(g, r - 1) + cut], back.at[(g, NY - r) + cut], at_y(r)
                )

    def weighted(k, start, size):
        order = BLOCKS.index(k)
        g, at = order // PER, pl.ds(order % PER * row_count, row_count)
        tags = rows[pl.ds(order * row_count, row_count), pl.ds(main, TAG)].astype(F32)
        lanes = lax.broadcasted_iota(jnp.int32, (row_count, TAG), 1) % EXPERTS
        total = jnp.zeros((row_count, size), F32)
        for j in range(NY):
            expert = z * NY + (y + j) % NY
            scale = jnp.sum(jnp.where(lanes == expert, tags, 0.0), axis=1, keepdims=True)
            fetched = jnp.dot(choose_t[g, j, at, :], back[g, j, :, pl.ds(start, size)], preferred_element_type=F32)
            total = total + scale * fetched
        return total

    def returned(g, n):
        for j in range(1, NY):
            from_expert[g, j, n].wait_recv()

    def piece_of(ref, place, n):
        return ref.at[place, pl.ds(0, row_count), pl.ds(*COLUMNS[n])]

    sums = {}

    def far_sums(n):
        returned(1, n)
        cut = pl.ds(*COLUMNS[n])
        part[4, :, cut] = weighted(4, *COLUMNS[n]).astype(BF16)
        sums[3, n] = go(piece_of(part, 4, n), piece_of(came, 0, n), at_z(1))
        part[5, :, cut] = weighted(5, *COLUMNS[n]).astype(BF16)
        sums[6, n] = go(piece_of(part, 5, n), piece_of(came, 1, n), at_z(-1))

    def far_ends(n):
        cut = pl.ds(*COLUMNS[n])
        mine = weighted(3, *COLUMNS[n])
        sums[3, n].wait_recv()
        part[3, :, cut] = (mine + came[0, :, cut].astype(F32)).astype(BF16)
        sums[0, 3, n] = go(piece_of(part, 3, n), piece_of(came, 2, n), at_z(3))
        mine = weighted(6, *COLUMNS[n])
        sums[6, n].wait_recv()
        part[6, :, cut] = (mine + came[1, :, cut].astype(F32)).astype(BF16)
        sums[0, 6, n] = go(piece_of(part, 6, n), piece_of(came, 3, n), at_z(-2))

    def near_sums():
        returned(0, 0)
        returned(0, 1)
        part[2] = weighted(2, 0, width).astype(BF16)
        sums[0, 2] = go(part.at[2], came.at[4], at_z(2))
        part[1] = weighted(1, 0, width).astype(BF16)
        sums[0, 1] = go(part.at[1], came.at[5], at_z(1))
        part[7] = weighted(7, 0, width).astype(BF16)
        sums[0, 7] = go(part.at[7], came.at[6], at_z(-1))

    def finish():
        for k in (1, 7, 2):
            sums[0, k].wait_recv()
        for n, columns in enumerate(COLUMNS):
            cut = pl.ds(*columns)
            total = weighted(0, *columns)
            for place in (5, 6, 4):
                total = total + came[place, :, cut].astype(F32)
            sums[0, 6, n].wait_recv()
            total = total + came[3, :, cut].astype(F32)
            sums[0, 3, n].wait_recv()
            mixed[:, cut] = (total + came[2, :, cut].astype(F32)).astype(BF16)

    endings = {
        "s0": near_sums, "s1": lambda: far_sums(0), "s4": lambda: far_sums(1),
        "s3": lambda: far_ends(0), "s5": lambda: far_ends(1), "s2": finish,
    }
    stages = {
        "q": pick_early, "h": early_share, "a": x_start, "b": x_forward, "c": x_last, "m": first_half,
        "e": hidden_forward, "d": hidden_last, "f": second_half,
    }
    for word in SCHEDULE:
        kind, number = word[0], int(word[1:])
        if kind == "z":
            hop(rows, "main", number)
        elif kind == "g":
            early_hop(number)
        elif kind == "p":
            pick(number // 4, number % 4)
        elif kind == "s":
            endings[word]()
        else:
            stages[kind](number // 4, number % 4)
    for copy in sent:
        copy.wait_send()


COPIES = 220


def shards(tokens, gate_weight, up_weight, down_weight, routes, route_weights, slot_counts):
    row_count, width = tokens.shape
    _, depth, units = gate_weight.shape
    hidden = down_weight.shape[1]
    vmem = pl.BlockSpec(memory_space=pltpu.VMEM)
    hbm = pl.BlockSpec(memory_space=pl.ANY)
    span = PER * row_count
    main = width - EARLY
    return pl.pallas_call(
        kernel,
        out_shape=jax.ShapeDtypeStruct((row_count, width), BF16),
        in_specs=[vmem] * 4 + [hbm] * 3,
        out_specs=vmem,
        scratch_shapes=[
            pltpu.VMEM((NZ * row_count, main + TAG), BF16),
            pltpu.VMEM((NZ * row_count, NX * EARLY), BF16),
            pltpu.VMEM((depth, units), BF16),
            pltpu.VMEM((depth, units), BF16),
            pltpu.VMEM((hidden, width), BF16),
            pltpu.VMEM((TAG, span), F32),
            pltpu.VMEM((G, NY, Q, span), BF16),
            pltpu.VMEM((G, NY, span, Q), BF16),
            pltpu.VMEM((G, NY - 1, Q, main), BF16),
            pltpu.VMEM((G, NY - 1, Q, NX * EARLY), BF16),
            pltpu.VMEM((G, NX, 2, NY * Q, main), BF16),
            pltpu.VMEM((G, 2, NY * Q, NX * EARLY), BF16),
            pltpu.VMEM((G, NX, 2, NY * Q, units), BF16),
            pltpu.VMEM((G, NY - 1, Q, width), BF16),
            pltpu.VMEM((G, NY, Q, width), BF16),
            pltpu.VMEM((NZ, row_count, width), BF16),
            pltpu.VMEM((NZ - 1, row_count, width), BF16),
            pltpu.SemaphoreType.DMA((3,)),
            pltpu.SemaphoreType.DMA((COPIES,)),
            pltpu.SemaphoreType.DMA((COPIES,)),
        ],
        compiler_params=pltpu.CompilerParams(
            collective_id=0, has_side_effects=True, vmem_limit_bytes=60 * 1024 * 1024
        ),
    )(tokens, routes.T, route_weights.T, slot_counts[None, :], gate_weight, up_weight, down_weight)


def solution(mesh):
    placed = (
        P("ep", "dp"),
        P("ep", None, "dp"),
        P("ep", None, "dp"),
        P("ep", None, "dp"),
        P("ep", None),
        P("ep", None),
        P("ep"),
    )
    return jax.shard_map(
        shards, mesh=mesh, in_specs=placed, out_specs=P("ep", "dp"), check_vma=False
    )
```

```python
import jax
import jax.numpy as jnp
from jax import lax
from jax.experimental import pallas as pl
from jax.experimental.pallas import tpu as pltpu
from jax.sharding import PartitionSpec as P

MESH = pl.DeviceIdType.MESH
NZ, NY, NX = 8, 4, 4
CAP = 20
EXPERTS = 32
TAG = 128
EARLY = 256
GROUPS = ((0, 1, 7, 2), (6, 3, 5, 4))
BLOCKS = GROUPS[0] + GROUPS[1]
G = len(GROUPS)
PER = len(GROUPS[0])
Q = PER * CAP
SIDE = (0, 1, 3, 2)
MARK = 1024.0
COLUMNS = ((0, 512), (512, 384))
DIRECT = ((1, 2), (1, 3),)
RING_DIRECT = ()
F32 = jnp.float32
BF16 = jnp.bfloat16
SCHEDULE = (
    "g0", "z1", "g1", "z2", "p0", "a0", "p3", "p1", "p2", "g2", "q0", "q2", "q1", "q3", "h0", "a1", "z3",
    "b0", "a2", "a3", "g3", "z4", "p4", "p7", "p5", "p6", "b1", "h3", "c0", "g4", "q4", "q7", "q6", "q5",
    "a4", "h4", "m0", "b2", "h2", "h1", "b3", "c1", "a5", "m1", "b4", "e0", "a6", "c2", "c3", "h5", "m2",
    "b5", "m3", "e1", "h7", "h6", "c4", "a7", "d0", "m4", "f0", "b6", "c5", "e2", "m5", "d1", "e3", "f1",
    "b7", "e4", "d3", "c6", "f3", "d2", "e5", "m6", "d4", "c7", "f2", "f4", "d5", "m7", "e6", "f5", "d6",
    "f6", "e7", "s0", "d7", "f7", "s1", "s4", "s3", "s5", "s2",
)


def kernel(
    tokens, routes, weights, counts, gate, up, down, mixed,
    rows, early, gate_w, up_w, down_w, place_t, choose, choose_t, picked, picked_e, gath, gath_e, hid, outs, back, part, came,
    load_sem, send, recv,
):
    row_count, width = tokens.shape
    units = gate_w.shape[1]
    top = routes.shape[0]
    span = PER * row_count
    main = width - EARLY
    ep, dp = lax.axis_index("ep"), lax.axis_index("dp")
    z, y, x, core = ep // NY, ep % NY, dp // 2, dp % 2
    used = [0]
    sent = []

    def at_z(k):
        return (((z + k) % NZ) * NY + y, dp)

    def at_y(k):
        return (z * NY + (y + k) % NY, dp)

    def at_x(k):
        return (ep, ((x + k) % NX) * 2 + core)

    other = (ep, x * 2 + 1 - core)

    def go(src, dst, device):
        n = used[0]
        used[0] += 1
        copy = pltpu.make_async_remote_copy(
            src_ref=src, dst_ref=dst, send_sem=send.at[n], recv_sem=recv.at[n],
            device_id=device, device_id_type=MESH,
        )
        copy.start()
        sent.append(copy)
        return copy

    loads = [
        pltpu.make_async_copy(gate.at[0], gate_w, load_sem.at[0]),
        pltpu.make_async_copy(up.at[0], up_w, load_sem.at[1]),
        pltpu.make_async_copy(down.at[0], down_w, load_sem.at[2]),
    ]
    for load in loads:
        load.start()

    barrier = pltpu.get_barrier_semaphore()
    partners = [at_z(1), at_z(-1), at_z(2), at_z(-2), at_z(3), at_z(-3), at_x(2), at_y(1), at_y(2), at_y(3), at_x(1), at_x(-1), other]
    for device in partners:
        pl.semaphore_signal(barrier, inc=1, device_id=device, device_id_type=MESH)

    expert_at = lax.broadcasted_iota(jnp.int32, (TAG, row_count), 0) % EXPERTS
    dense = jnp.zeros((TAG, row_count), F32)
    for k in range(top):
        live = jnp.logical_and(expert_at == routes[k : k + 1, :], counts[...] > k)
        dense = dense + jnp.where(live, weights[k : k + 1, :], 0.0)
    dense = jnp.concatenate([dense, jnp.zeros((TAG, TAG - row_count), F32)], axis=1).T[:row_count]
    high = dense.astype(BF16).astype(F32)
    middle = (dense - high).astype(BF16).astype(F32)
    low = dense - high - middle
    term = lax.broadcasted_iota(jnp.int32, (row_count, TAG), 1) // EXPERTS
    tag = jnp.where(term == 0, high, jnp.where(term == 1, middle, jnp.where(term == 2, low, 0.0)))
    rows[pl.ds(0, row_count), pl.ds(main, TAG)] = tag.astype(BF16)
    rows[pl.ds(0, row_count), pl.ds(0, main)] = tokens[:, :main]
    early[pl.ds(0, row_count), pl.ds(0, EARLY)] = tokens[:, main:]

    pl.semaphore_wait(barrier, len(partners))

    half_rows = row_count // 2

    def block(ref, k, h):
        return ref.at[pl.ds(BLOCKS.index(k) * row_count + h * half_rows, half_rows)]

    moves = {}

    def onward(ref, name, k, h, step):
        to = (k + step) % NZ
        moves[name, to, h] = go(block(ref, k, h), block(ref, to, h), at_z(-step))

    def first_hop(ref, name):
        for h in (0, 1):
            onward(ref, name, 0, h, 1)
            onward(ref, name, 0, 1 - h, -1)

    def hop(ref, name, k):
        for h in (0, 1):
            moves[name, k, h].wait_recv()
            if k < NZ // 2:
                if k < NZ // 2 - 1 or h == 0:
                    onward(ref, name, k, h, 1)
                moves[name, NZ - k, 1 - h].wait_recv()
                if k < NZ // 2 - 1 or h == 0:
                    onward(ref, name, NZ - k, 1 - h, -1)

    first_hop(rows, "main")

    own_rows = pl.ds(0, row_count)

    def early_at(dx):
        return pl.ds(dx * EARLY, EARLY)

    own_early = early.at[own_rows, early_at(0)]
    gathered = [go(own_early, early.at[own_rows, early_at(NX - step)], at_x(step)) for step in (1, 3, 2)]

    def early_hop(k):
        if k == 0:
            for copy in gathered:
                copy.wait_recv()
            first_hop(early, "early")
        else:
            hop(early, "early", k)

    def group_tags(g):
        return rows[pl.ds(g * span, span), pl.ds(main, TAG)]

    def places(g):
        taken = jnp.where(group_tags(g).astype(F32) > 0.0, 1.0, 0.0).astype(BF16)
        first = lax.broadcasted_iota(jnp.int32, (span, span), 0)
        second = lax.broadcasted_iota(jnp.int32, (span, span), 1)
        ahead = jnp.where(first < second, 1.0, jnp.where(first == second, MARK, 0.0)).astype(BF16)
        place_t[...] = lax.dot_general(taken, ahead, (((0,), (0,)), ((), ())), preferred_element_type=F32)
        behind = jnp.where(second < first, 1.0, jnp.where(first == second, MARK, 0.0)).astype(BF16)
        place = jnp.dot(behind, taken, preferred_element_type=F32)
        lanes = lax.broadcasted_iota(jnp.int32, (span, TAG), 1)
        slot = lax.broadcasted_iota(jnp.int32, (Q, span), 0).astype(F32) + MARK
        slot_t = lax.broadcasted_iota(jnp.int32, (span, Q), 1).astype(F32) + MARK
        for j in range(NY):
            expert = z * NY + (y + j) % NY
            choose[g, j] = jnp.where(place_t[pl.ds(expert, 1), :] == slot, 1.0, 0.0).astype(BF16)
            column = jnp.sum(jnp.where(lanes == expert, place, 0.0), axis=1, keepdims=True)
            choose_t[g, j] = jnp.where(column == slot_t, 1.0, 0.0).astype(BF16)

    def spot(q):
        return pl.ds(q * Q, Q)

    to_expert = {}

    def pick(g, j):
        if j == 0:
            places(g)
        source = rows[pl.ds(g * span, span), pl.ds(0, main)]
        chosen = jnp.dot(choose[g, j], source, preferred_element_type=F32).astype(BF16)
        q = SIDE.index((NY - j) % NY)
        if j == 0:
            gath[g, 0, 0, spot(q), :] = chosen
        else:
            picked[g, j - 1] = chosen
            to_expert[g, q] = go(picked.at[g, j - 1], gath.at[g, 0, 0, spot(q)], at_y(j))

    early_to = {}
    early_shared = {}

    def pick_early(g, j):
        chosen = jnp.dot(choose[g, j], early[pl.ds(g * span, span), :], preferred_element_type=F32).astype(BF16)
        q = SIDE.index((NY - j) % NY)
        if j == 0:
            gath_e[g, 0, spot(q), :] = chosen
        else:
            picked_e[g, j - 1] = chosen
            early_to[g, q] = go(picked_e.at[g, j - 1], gath_e.at[g, 0, spot(q)], at_y(j))

    def early_share(g, q):
        if (g, q) in early_to:
            early_to[g, q].wait_recv()
        early_shared[g, q] = go(gath_e.at[g, 0, spot(q)], gath_e.at[g, 1, spot(q)], other)

    ring = {}

    def x_start(g, q):
        if (g, q) in to_expert:
            to_expert[g, q].wait_recv()
        at = spot(q)
        mine = gath.at[g, 0, 0, at]
        ring[g, q, 3, 0] = go(mine, gath.at[g, 3, 0, at], at_x(1))
        ring[g, q, 1, 0] = go(mine, gath.at[g, 1, 0, at], at_x(-1))
        if (g, q) in RING_DIRECT:
            ring[g, q, 2, 0] = go(mine, gath.at[g, 2, 0, at], at_x(2))
        ring[g, q, 0, 1] = go(mine, gath.at[g, 0, 1, at], other)

    def share(g, q, dx):
        at = spot(q)
        ring[g, q, dx, 1] = go(gath.at[g, dx, 0, at], gath.at[g, dx, 1, at], other)

    def x_forward(g, q):
        at = spot(q)
        ring[g, q, 3, 0].wait_recv()
        if (g, q) not in RING_DIRECT and q % 2 == 0:
            ring[g, q, 2, 0] = go(gath.at[g, 3, 0, at], gath.at[g, 2, 0, at], at_x(1))
        share(g, q, 3)
        ring[g, q, 1, 0].wait_recv()
        if (g, q) not in RING_DIRECT and q % 2 == 1:
            ring[g, q, 2, 0] = go(gath.at[g, 1, 0, at], gath.at[g, 2, 0, at], at_x(-1))
        share(g, q, 1)

    def x_last(g, q):
        ring[g, q, 2, 0].wait_recv()
        share(g, q, 2)

    STEPS = ((0, 0), (3, 0), (1, 0), (2, 0), (0, 1), (3, 1), (1, 1), (2, 1))
    waited = []

    def slice_at(dx, dc):
        return ((x + dx) % NX) * 2 + (core if dc == 0 else 1 - core)

    hops = {}

    def first_half(g, q):
        if not waited:
            waited.append(1)
            for load in loads:
                load.wait()
        at = spot(q)
        early_shared[g, q].wait_recv()
        gate_acc = jnp.zeros((Q, units), F32)
        up_acc = jnp.zeros((Q, units), F32)
        for dx, dc in STEPS:
            deep = pl.ds(pl.multiple_of(slice_at(dx, dc) * width + main, 128), EARLY)
            piece = gath_e[g, dc, at, early_at(dx)]
            gate_acc = gate_acc + jnp.dot(piece, gate_w[deep, :], preferred_element_type=F32)
            up_acc = up_acc + jnp.dot(piece, up_w[deep, :], preferred_element_type=F32)
        for dx, dc in STEPS:
            if dc == 1:
                ring[g, q, dx, 1].wait_recv()
            deep = pl.ds(pl.multiple_of(slice_at(dx, dc) * width, width), main)
            piece = gath[g, dx, dc, at, :]
            gate_acc = gate_acc + jnp.dot(piece, gate_w[deep, :], preferred_element_type=F32)
            up_acc = up_acc + jnp.dot(piece, up_w[deep, :], preferred_element_type=F32)
        hid[g, 0, 0, at, :] = (gate_acc / (1.0 + jnp.exp(-gate_acc)) * up_acc).astype(BF16)
        mine = hid.at[g, 0, 0, at]
        hops[g, q, 3, 0] = go(mine, hid.at[g, 3, 0, at], at_x(1))
        hops[g, q, 1, 0] = go(mine, hid.at[g, 1, 0, at], at_x(-1))
        if (g, q) in DIRECT:
            hops[g, q, 2, 0] = go(mine, hid.at[g, 2, 0, at], at_x(2))
        hops[g, q, 0, 1] = go(mine, hid.at[g, 0, 1, at], other)

    def hidden_forward(g, q):
        at = spot(q)
        for dx, step in ((3, 1), (1, -1)):
            hops[g, q, dx, 0].wait_recv()
            if (g, q) not in DIRECT and q % 2 == (dx == 1):
                hops[g, q, 2, 0] = go(hid.at[g, dx, 0, at], hid.at[g, 2, 0, at], at_x(step))
            hops[g, q, dx, 1] = go(hid.at[g, dx, 0, at], hid.at[g, dx, 1, at], other)

    def hidden_last(g, q):
        at = spot(q)
        hops[g, q, 2, 0].wait_recv()
        hops[g, q, 2, 1] = go(hid.at[g, 2, 0, at], hid.at[g, 2, 1, at], other)

    from_expert = {}

    def second_half(g, q):
        at = spot(q)
        acc = jnp.zeros((Q, width), F32)
        for dx, dc in STEPS:
            if dc == 1:
                hops[g, q, dx, 1].wait_recv()
            deep = pl.ds(pl.multiple_of(slice_at(dx, dc) * units, units), units)
            acc = acc + jnp.dot(hid[g, dx, dc, at, :], down_w[deep, :], preferred_element_type=F32)
        r = SIDE[q]
        if r == 0:
            back[g, 0] = acc.astype(BF16)
        else:
            outs[g, r - 1] = acc.astype(BF16)
            for n, columns in enumerate(COLUMNS):
                cut = pl.ds(0, Q), pl.ds(*columns)
                from_expert[g, NY - r, n] = go(
                    outs.at[(g, r - 1) + cut], back.at[(g, NY - r) + cut], at_y(r)
                )

    def weighted(k, start, size):
        order = BLOCKS.index(k)
        g, at = order // PER, pl.ds(order % PER * row_count, row_count)
        tags = rows[pl.ds(order * row_count, row_count), pl.ds(main, TAG)].astype(F32)
        lanes = lax.broadcasted_iota(jnp.int32, (row_count, TAG), 1) % EXPERTS
        total = jnp.zeros((row_count, size), F32)
        for j in range(NY):
            expert = z * NY + (y + j) % NY
            scale = jnp.sum(jnp.where(lanes == expert, tags, 0.0), axis=1, keepdims=True)
            fetched = jnp.dot(choose_t[g, j, at, :], back[g, j, :, pl.ds(start, size)], preferred_element_type=F32)
            total = total + scale * fetched
        return total

    def returned(g, n):
        for j in range(1, NY):
            from_expert[g, j, n].wait_recv()

    def piece_of(ref, place, n):
        return ref.at[place, pl.ds(0, row_count), pl.ds(*COLUMNS[n])]

    sums = {}

    def far_sums(n):
        returned(1, n)
        cut = pl.ds(*COLUMNS[n])
        part[4, :, cut] = weighted(4, *COLUMNS[n]).astype(BF16)
        sums[3, n] = go(piece_of(part, 4, n), piece_of(came, 0, n), at_z(1))
        part[5, :, cut] = weighted(5, *COLUMNS[n]).astype(BF16)
        sums[6, n] = go(piece_of(part, 5, n), piece_of(came, 1, n), at_z(-1))

    def far_ends(n):
        cut = pl.ds(*COLUMNS[n])
        mine = weighted(3, *COLUMNS[n])
        sums[3, n].wait_recv()
        part[3, :, cut] = (mine + came[0, :, cut].astype(F32)).astype(BF16)
        sums[0, 3, n] = go(piece_of(part, 3, n), piece_of(came, 2, n), at_z(3))
        mine = weighted(6, *COLUMNS[n])
        sums[6, n].wait_recv()
        part[6, :, cut] = (mine + came[1, :, cut].astype(F32)).astype(BF16)
        sums[0, 6, n] = go(piece_of(part, 6, n), piece_of(came, 3, n), at_z(-2))

    def near_sums():
        returned(0, 0)
        returned(0, 1)
        part[2] = weighted(2, 0, width).astype(BF16)
        sums[0, 2] = go(part.at[2], came.at[4], at_z(2))
        part[1] = weighted(1, 0, width).astype(BF16)
        sums[0, 1] = go(part.at[1], came.at[5], at_z(1))
        part[7] = weighted(7, 0, width).astype(BF16)
        sums[0, 7] = go(part.at[7], came.at[6], at_z(-1))

    def finish():
        for k in (1, 7, 2):
            sums[0, k].wait_recv()
        for n, columns in enumerate(COLUMNS):
            cut = pl.ds(*columns)
            total = weighted(0, *columns)
            for place in (5, 6, 4):
                total = total + came[place, :, cut].astype(F32)
            sums[0, 6, n].wait_recv()
            total = total + came[3, :, cut].astype(F32)
            sums[0, 3, n].wait_recv()
            mixed[:, cut] = (total + came[2, :, cut].astype(F32)).astype(BF16)

    endings = {
        "s0": near_sums, "s1": lambda: far_sums(0), "s4": lambda: far_sums(1),
        "s3": lambda: far_ends(0), "s5": lambda: far_ends(1), "s2": finish,
    }
    stages = {
        "q": pick_early, "h": early_share, "a": x_start, "b": x_forward, "c": x_last, "m": first_half,
        "e": hidden_forward, "d": hidden_last, "f": second_half,
    }
    for word in SCHEDULE:
        kind, number = word[0], int(word[1:])
        if kind == "z":
            hop(rows, "main", number)
        elif kind == "g":
            early_hop(number)
        elif kind == "p":
            pick(number // 4, number % 4)
        elif kind == "s":
            endings[word]()
        else:
            stages[kind](number // 4, number % 4)
    for copy in sent:
        copy.wait_send()


COPIES = 220


def shards(tokens, gate_weight, up_weight, down_weight, routes, route_weights, slot_counts):
    row_count, width = tokens.shape
    _, depth, units = gate_weight.shape
    hidden = down_weight.shape[1]
    vmem = pl.BlockSpec(memory_space=pltpu.VMEM)
    hbm = pl.BlockSpec(memory_space=pl.ANY)
    span = PER * row_count
    main = width - EARLY
    return pl.pallas_call(
        kernel,
        out_shape=jax.ShapeDtypeStruct((row_count, width), BF16),
        in_specs=[vmem] * 4 + [hbm] * 3,
        out_specs=vmem,
        scratch_shapes=[
            pltpu.VMEM((NZ * row_count, main + TAG), BF16),
            pltpu.VMEM((NZ * row_count, NX * EARLY), BF16),
            pltpu.VMEM((depth, units), BF16),
            pltpu.VMEM((depth, units), BF16),
            pltpu.VMEM((hidden, width), BF16),
            pltpu.VMEM((TAG, span), F32),
            pltpu.VMEM((G, NY, Q, span), BF16),
            pltpu.VMEM((G, NY, span, Q), BF16),
            pltpu.VMEM((G, NY - 1, Q, main), BF16),
            pltpu.VMEM((G, NY - 1, Q, NX * EARLY), BF16),
            pltpu.VMEM((G, NX, 2, NY * Q, main), BF16),
            pltpu.VMEM((G, 2, NY * Q, NX * EARLY), BF16),
            pltpu.VMEM((G, NX, 2, NY * Q, units), BF16),
            pltpu.VMEM((G, NY - 1, Q, width), BF16),
            pltpu.VMEM((G, NY, Q, width), BF16),
            pltpu.VMEM((NZ, row_count, width), BF16),
            pltpu.VMEM((NZ - 1, row_count, width), BF16),
            pltpu.SemaphoreType.DMA((3,)),
            pltpu.SemaphoreType.DMA((COPIES,)),
            pltpu.SemaphoreType.DMA((COPIES,)),
        ],
        compiler_params=pltpu.CompilerParams(
            collective_id=0, has_side_effects=True, vmem_limit_bytes=60 * 1024 * 1024
        ),
    )(tokens, routes.T, route_weights.T, slot_counts[None, :], gate_weight, up_weight, down_weight)


def solution(mesh):
    placed = (
        P("ep", "dp"),
        P("ep", None, "dp"),
        P("ep", None, "dp"),
        P("ep", None, "dp"),
        P("ep", None),
        P("ep", None),
        P("ep"),
    )
    return jax.shard_map(
        shards, mesh=mesh, in_specs=placed, out_specs=P("ep", "dp"), check_vma=False
    )
```
